512 devices in a mesh: lat: 8 (over x, y_lo), lon: 16 (over z, core), ch: 4 (over y_hi).
Axes of the slice: x: 4, y: 8 (y_hi: 4, y_lo: 2; y = y_hi * 2 + y_lo), z: 8, core: 2. Of those that a mesh axis runs over, the one named last changes fastest.
Arguments:
- features: bfloat16 [1, 56, 384, 1024], P(None, 'lat', 'lon', 'ch'), may hold values from -6 to 6
- kernel_one: bfloat16 [3, 3, 4, 256, 1024], P(None, None, 'ch', 'lon'), may hold values from -0.0625 to 0.0625
- bias_one: float32 [1024], P('ch'), may hold values from -3 to 3
- kernel_two: bfloat16 [3, 3, 4, 256, 1024], P(None, None, 'ch', 'lon'), may hold values from -0.0625 to 0.0625
- bias_two: float32 [1024], P('ch'), may hold values from -3 to 3
Outputs:
- outputs: bfloat16 [1, 56, 384, 1024], P(None, 'lat', 'lon', 'ch')
The draws below stay inside these ranges and needn't reach their ends.
All inputs are finite; a program needn't handle non-finite values.
Results may differ from the reference program's by a relative error of at most 0.01.
Values may be sent and summed in bfloat16 or wider, within the bound.
No kernel may reach another device: no remote copies, remote signals or barrier semaphores. Data moves between devices by JAX's collectives and lax.ppermute only.
A program may use at most 64 MiB of HBM per device.

```python
import jax
import jax.numpy as jnp
from jax import lax

C = 1024
BATCH = 1
NLAT = 56
NLON = 384
N_CH = 4


def block_levels(own_key, shape, pieces, low, top_value):
    factor_of, own = 1.0, jax.random.fold_in(own_key, 6)
    for position, blocks in pieces:
        steps = jnp.exp(jax.random.uniform(jax.random.fold_in(own, position), (blocks,), jnp.float32, low / len(pieces), top_value / len(pieces)))
        factor_of = factor_of * jnp.repeat(steps, shape[position] // blocks).reshape([-1 if axis == position else 1 for axis in range(len(shape))])
    return factor_of


def normal_values(own_key, shape, deviation, bound, cuts=(), held_as=jnp.bfloat16):
    level = block_levels(own_key, shape, cuts, -0.22, 0.18) if cuts else 1.0
    entries = jax.random.normal(own_key, shape, jnp.float32) * deviation * level
    return jnp.minimum(jnp.maximum(entries, -bound), bound).astype(held_as)


def setup_inputs(seed: int = 0) -> dict:
    key_of = jax.random.split(jax.random.key(seed), 6)
    return {
        "features": normal_values(key_of[0], (BATCH, NLAT, NLON, C), 1.0, 6.0, ((1, 8), (2, 16), (3, 4))),
        "kernel_one": normal_values(key_of[1], (3, 3, N_CH, C // N_CH, C), (9 * C) ** -0.5, 0.0625, ((2, 4), (3, 16))),
        "bias_one": normal_values(key_of[2], (C,), 0.5, 3.0, ((0, 4),), jnp.float32),
        "kernel_two": normal_values(key_of[3], (3, 3, N_CH, C // N_CH, C), (9 * C) ** -0.5, 0.0625, ((2, 4), (3, 16))),
        "bias_two": normal_values(key_of[4], (C,), 0.5, 3.0, ((0, 4),), jnp.float32),
    }


skip_scale = 0.7071067811865476


def apply_taps(padded, kernel):
    count_items = padded.shape[0]
    height = padded.shape[1] - 2
    breadth = padded.shape[2] - 2
    channels = padded.shape[3]
    accumulated = jnp.zeros((count_items * height * breadth, kernel.shape[3]), jnp.float32)
    for row_off in range(3):
        for col_off in range(3):
            window = padded[:, row_off:row_off + height, col_off:col_off + breadth].reshape(-1, channels)
            accumulated = accumulated + jnp.dot(window, kernel[row_off, col_off], preferred_element_type=jnp.float32)
    return accumulated.reshape(count_items, height, breadth, kernel.shape[3])


def fold_pad(source):
    half_turn = source.shape[2] // 2
    top_row = jnp.roll(source[:, :1], half_turn, axis=2)
    low_row = jnp.roll(source[:, -1:], half_turn, axis=2)
    banded = jnp.concatenate([top_row, source, low_row], axis=1)
    return jnp.concatenate([banded[:, :, -1:], banded, banded[:, :, :1]], axis=2)


def conv_sum(activation, kernel_full, bias_vec):
    kernel = kernel_full.reshape(3, 3, C, C)
    padded = fold_pad(activation)
    width_group = C // N_CH

    def group_step(running, group_idx):
        start_idx = (group_idx * width_group).astype(jnp.int32)
        piece_in = lax.dynamic_slice_in_dim(padded, start_idx, width_group, 3)
        piece_kernel = lax.dynamic_slice_in_dim(kernel, start_idx, width_group, 2)
        partial_value = apply_taps(piece_in, piece_kernel).astype(jnp.bfloat16)
        partial_value = lax.optimization_barrier(partial_value)
        return running + partial_value.astype(jnp.float32), None

    initial = jnp.zeros(activation.shape[:3] + (C,), jnp.float32)
    summed, unused = lax.scan(group_step, initial, jnp.arange(N_CH, dtype=jnp.int32))
    return summed + bias_vec.astype(jnp.float32)


def reference(features, kernel_one, bias_one, kernel_two, bias_two):
    act_zero = jax.nn.silu(features.astype(jnp.float32)).astype(jnp.bfloat16)
    hidden = conv_sum(act_zero, kernel_one, bias_one)
    act_one = jax.nn.silu(hidden).astype(jnp.bfloat16)
    second = conv_sum(act_one, kernel_two, bias_two)
    return ((features.astype(jnp.float32) + second) * skip_scale).astype(jnp.bfloat16)
```

```python
import jax
import jax.numpy as jnp
from jax import lax
from jax.sharding import Mesh, PartitionSpec as P

skip_scale = 0.7071067811865476
AXES = ("x", "ylo", "z", "core", "ch")
LAT, LON, POLE = ("x", "ylo"), ("z", "core"), ("x", "ylo", "z", "core")


def silu(v):
    return jax.nn.silu(v.astype(jnp.float32)).astype(jnp.bfloat16)


def half_of(kernel, ylo):
    taps, rows, groups = 9, kernel.shape[3], 4
    flat = kernel.reshape(taps, rows, kernel.shape[4])
    width = kernel.shape[4] // groups
    low = [flat[:, :, g * width : g * width + width // 2] for g in range(groups)]
    high = [flat[:, :, g * width + width // 2 : (g + 1) * width] for g in range(groups)]
    return jnp.where(ylo == 0, jnp.concatenate(low, 2), jnp.concatenate(high, 2))


def lon_halo(block, width, lon):
    up = [(i, (i + 1) % lon) for i in range(lon)]
    down = [(j, i) for i, j in up]
    before = lax.ppermute(block[:, -width:], LON, up)
    after = lax.ppermute(block[:, :width], LON, down)
    return jnp.concatenate([before, block, after], axis=1)


def lat_pairs(lat, lon):
    pairs = []
    for i in range(lat):
        for j in range(lon):
            k = i - 1 if i % 2 == 0 else i + 1
            to = (k, j) if 0 <= k < lat else (i, (j + lon // 2) % lon)
            pairs.append((i * lon + j, to[0] * lon + to[1]))
    return pairs


def region(block, lat, lon):
    x, ylo = lax.axis_index("x"), lax.axis_index("ylo")
    wide = lon_halo(block, 2, lon)
    sent = jnp.where(ylo == 0, wide[:2], wide[-2:])
    came = lax.ppermute(sent, POLE, lat_pairs(lat, lon))
    at_pole = jnp.logical_or((x == 0) & (ylo == 0), (x == lat // 2 - 1) & (ylo == 1))
    came = jnp.where(at_pole, came[::-1], came)
    nine = jnp.where(
        ylo == 0, jnp.concatenate([came, wide]), jnp.concatenate([wide, came])
    )
    other = lax.ppermute(nine, "ylo", [(0, 1), (1, 0)])
    return jnp.concatenate([jnp.where(ylo == 0, nine, other), jnp.where(ylo == 0, other, nine)])


def conv(rows_of, columns, kernel):
    windows = [rows_of(a)[:, e : e + columns] for a in range(3) for e in range(3)]
    stacked = jnp.concatenate(windows, axis=2)
    flat = stacked.reshape(-1, stacked.shape[2])
    return jnp.dot(flat, kernel, preferred_element_type=jnp.float32).astype(jnp.bfloat16)


def body(features, kernel_one, bias_one, kernel_two, bias_two):
    lat = lax.axis_size("x") * lax.axis_size("ylo")
    lon = lax.axis_size("z") * lax.axis_size("core")
    x, ylo = lax.axis_index("x"), lax.axis_index("ylo")
    own = features[0]
    height, breadth, width = own.shape

    both = jnp.stack([half_of(kernel_one, ylo), half_of(kernel_two, ylo)])
    both = lax.all_gather(both, LON, axis=2, tiled=True)
    both = both.reshape(2, 9 * width, both.shape[3])

    ext = region(silu(own), lat, lon)
    top, bottom = x == 0, x == lax.axis_size("x") - 1
    last = ext.shape[0] - 1

    def rows_of(a):
        first = jnp.where(top, ext[2 - a : 3 - a], ext[a : a + 1])
        final = jnp.where(bottom, ext[last - a : last - a + 1], ext[last - 2 + a : last - 1 + a])
        return jnp.concatenate([first, ext[a + 1 : last - 2 + a], final])

    partial_one = conv(rows_of, breadth + 2, both[0])
    cells = partial_one.shape[0]
    partial_one = partial_one.reshape(cells, 4, width // 2).transpose(1, 0, 2)
    parts = lax.all_to_all(partial_one, "ch", 0, 0)
    hidden = parts.astype(jnp.float32).sum(0)
    hidden = hidden + jnp.where(ylo == 0, bias_one[: width // 2], bias_one[width // 2 :])
    mine = silu(hidden)
    other = lax.ppermute(mine, "ylo", [(0, 1), (1, 0)])
    act = jnp.concatenate(
        [jnp.where(ylo == 0, mine, other), jnp.where(ylo == 0, other, mine)], axis=1
    )
    act = act.reshape(2 * height + 2, breadth + 2, width)

    partial_two = conv(lambda a: act[a : a + 2 * height], breadth, both[1])
    partial_two = partial_two.reshape(2, height * breadth, 4, width // 2)
    partial_two = partial_two.transpose(0, 2, 1, 3).reshape(8, height * breadth, width // 2)
    parts = lax.all_to_all(partial_two, ("ylo", "ch"), 0, 0)
    second = parts.astype(jnp.float32).reshape(2, 4, height * breadth, width // 2).sum(1)
    second = jnp.concatenate([second[0], second[1]], axis=1) + bias_two
    second = second.reshape(height, breadth, width)
    return ((own.astype(jnp.float32) + second) * skip_scale).astype(jnp.bfloat16)[None]


def solution(mesh):
    lat, lon, ch = (mesh.shape[name] for name in ("lat", "lon", "ch"))
    fine = Mesh(mesh.devices.reshape(lat // 2, 2, lon // 2, 2, ch), AXES)
    field = P(None, LAT, LON, "ch")
    kernel = P(None, None, "ch", LON, None)
    return jax.shard_map(
        body,
        mesh=fine,
        in_specs=(field, kernel, P("ch"), kernel, P("ch")),
        out_specs=field,
        check_vma=False,
    )
```

```python
import jax
import jax.numpy as jnp
from jax import lax
from jax.sharding import Mesh, PartitionSpec as P

skip_scale = 0.7071067811865476
AXES = ("x", "ylo", "z", "core", "ch")
LAT, LON, POLE = ("x", "ylo"), ("z", "core"), ("x", "ylo", "z", "core")


def silu(v):
    return jax.nn.silu(v.astype(jnp.float32)).astype(jnp.bfloat16)


def half_of(kernel, ylo):
    taps, rows, groups = 9, kernel.shape[3], 4
    flat = kernel.reshape(taps, rows, kernel.shape[4])
    width = kernel.shape[4] // groups
    low = [flat[:, :, g * width : g * width + width // 2] for g in range(groups)]
    high = [flat[:, :, g * width + width // 2 : (g + 1) * width] for g in range(groups)]
    return jnp.where(ylo == 0, jnp.concatenate(low, 2), jnp.concatenate(high, 2))


def lon_halo(block, width, lon):
    up = [(i, (i + 1) % lon) for i in range(lon)]
    down = [(j, i) for i, j in up]
    before = lax.ppermute(block[:, -width:], LON, up)
    after = lax.ppermute(block[:, :width], LON, down)
    return jnp.concatenate([before, block, after], axis=1)


def lat_pairs(lat, lon):
    pairs = []
    for i in range(lat):
        for j in range(lon):
            k = i - 1 if i % 2 == 0 else i + 1
            to = (k, j) if 0 <= k < lat else (i, (j + lon // 2) % lon)
            pairs.append((i * lon + j, to[0] * lon + to[1]))
    return pairs


def region(block, lat, lon):
    x, ylo = lax.axis_index("x"), lax.axis_index("ylo")
    wide = lon_halo(block, 2, lon)
    sent = jnp.where(ylo == 0, wide[:2], wide[-2:])
    came = lax.ppermute(sent, POLE, lat_pairs(lat, lon))
    at_pole = jnp.logical_or((x == 0) & (ylo == 0), (x == lat // 2 - 1) & (ylo == 1))
    came = jnp.where(at_pole, came[::-1], came)
    nine = jnp.where(
        ylo == 0, jnp.concatenate([came, wide]), jnp.concatenate([wide, came])
    )
    other = lax.ppermute(nine, "ylo", [(0, 1), (1, 0)])
    return jnp.concatenate([jnp.where(ylo == 0, nine, other), jnp.where(ylo == 0, other, nine)])


def conv(rows_of, columns, kernel):
    windows = [rows_of(a)[:, e : e + columns] for a in range(3) for e in range(3)]
    stacked = jnp.concatenate(windows, axis=2)
    flat = stacked.reshape(-1, stacked.shape[2])
    return jnp.dot(flat, kernel, preferred_element_type=jnp.float32).astype(jnp.bfloat16)


def body(features, kernel_one, bias_one, kernel_two, bias_two):
    lat = lax.axis_size("x") * lax.axis_size("ylo")
    lon = lax.axis_size("z") * lax.axis_size("core")
    x, ylo = lax.axis_index("x"), lax.axis_index("ylo")
    own = features[0]
    height, breadth, width = own.shape

    both = [
        lax.all_gather(half_of(kernel, ylo), LON, axis=1, tiled=True).reshape(9 * width, -1)
        for kernel in (kernel_one, kernel_two)
    ]

    ext = region(silu(own), lat, lon)
    top, bottom = x == 0, x == lax.axis_size("x") - 1
    last = ext.shape[0] - 1

    def rows_of(a):
        first = jnp.where(top, ext[2 - a : 3 - a], ext[a : a + 1])
        final = jnp.where(bottom, ext[last - a : last - a + 1], ext[last - 2 + a : last - 1 + a])
        return jnp.concatenate([first, ext[a + 1 : last - 2 + a], final])

    partial_one = conv(rows_of, breadth + 2, both[0])
    cells = partial_one.shape[0]
    partial_one = partial_one.reshape(cells, 4, width // 2).transpose(1, 0, 2)
    parts = lax.all_to_all(partial_one, "ch", 0, 0)
    hidden = parts.astype(jnp.float32).sum(0)
    hidden = hidden + jnp.where(ylo == 0, bias_one[: width // 2], bias_one[width // 2 :])
    mine = silu(hidden)
    other = lax.ppermute(mine, "ylo", [(0, 1), (1, 0)])
    act = jnp.concatenate(
        [jnp.where(ylo == 0, mine, other), jnp.where(ylo == 0, other, mine)], axis=1
    )
    act = act.reshape(2 * height + 2, breadth + 2, width)

    partial_two = conv(lambda a: act[a : a + 2 * height], breadth, both[1])
    partial_two = partial_two.reshape(2, height * breadth, 4, width // 2)
    partial_two = partial_two.transpose(0, 2, 1, 3).reshape(8, height * breadth, width // 2)
    parts = lax.all_to_all(partial_two, ("ylo", "ch"), 0, 0)
    second = parts.astype(jnp.float32).reshape(2, 4, height * breadth, width // 2).sum(1)
    second = jnp.concatenate([second[0], second[1]], axis=1) + bias_two
    second = second.reshape(height, breadth, width)
    return ((own.astype(jnp.float32) + second) * skip_scale).astype(jnp.bfloat16)[None]


def solution(mesh):
    lat, lon, ch = (mesh.shape[name] for name in ("lat", "lon", "ch"))
    fine = Mesh(mesh.devices.reshape(lat // 2, 2, lon // 2, 2, ch), AXES)
    field = P(None, LAT, LON, "ch")
    kernel = P(None, None, "ch", LON, None)
    return jax.shard_map(
        body,
        mesh=fine,
        in_specs=(field, kernel, P("ch"), kernel, P("ch")),
        out_specs=field,
        check_vma=False,
    )
```

```python
import jax
import jax.numpy as jnp
from jax import lax
from jax.experimental import pallas as pl
from jax.sharding import Mesh, PartitionSpec as P

skip_scale = 0.7071067811865476
AXES = ("x", "ylo", "z", "core", "ch")
LAT, LON, POLE = ("x", "ylo"), ("z", "core"), ("x", "ylo", "z", "core")


def silu(v):
    return jax.nn.silu(v.astype(jnp.float32)).astype(jnp.bfloat16)


def half_of(kernel, ylo):
    taps, rows, groups = 9, kernel.shape[3], 4
    flat = kernel.reshape(taps, rows, kernel.shape[4])
    width = kernel.shape[4] // groups
    low = [flat[:, :, g * width : g * width + width // 2] for g in range(groups)]
    high = [flat[:, :, g * width + width // 2 : (g + 1) * width] for g in range(groups)]
    return jnp.where(ylo == 0, jnp.concatenate(low, 2), jnp.concatenate(high, 2))


def lon_halo(block, width, lon):
    up = [(i, (i + 1) % lon) for i in range(lon)]
    down = [(j, i) for i, j in up]
    before = lax.ppermute(block[:, -width:], LON, up)
    after = lax.ppermute(block[:, :width], LON, down)
    return jnp.concatenate([before, block, after], axis=1)


def lat_pairs(lat, lon):
    pairs = []
    for i in range(lat):
        for j in range(lon):
            k = i - 1 if i % 2 == 0 else i + 1
            to = (k, j) if 0 <= k < lat else (i, (j + lon // 2) % lon)
            pairs.append((i * lon + j, to[0] * lon + to[1]))
    return pairs


def region(block, lat, lon):
    x, ylo = lax.axis_index("x"), lax.axis_index("ylo")
    wide = lon_halo(block, 2, lon)
    sent = jnp.where(ylo == 0, wide[:2], wide[-2:])
    came = lax.ppermute(sent, POLE, lat_pairs(lat, lon))
    at_pole = jnp.logical_or((x == 0) & (ylo == 0), (x == lat // 2 - 1) & (ylo == 1))
    came = jnp.where(at_pole, came[::-1], came)
    nine = jnp.where(
        ylo == 0, jnp.concatenate([came, wide]), jnp.concatenate([wide, came])
    )
    other = lax.ppermute(nine, "ylo", [(0, 1), (1, 0)])
    return jnp.concatenate([jnp.where(ylo == 0, nine, other), jnp.where(ylo == 0, other, nine)])


def columns_of(rows_of, columns):
    windows = [rows_of(a)[:, e : e + columns] for a in range(3) for e in range(3)]
    stacked = jnp.concatenate(windows, axis=2)
    return stacked.reshape(-1, stacked.shape[2])


def taps_kernel(cells_ref, kernel_ref, out_ref):
    parts, blocks, size, lanes = out_ref.shape
    owners, _, taps, rows, _ = kernel_ref.shape
    depth = owners * rows
    total = None
    for t in range(taps):
        tap = kernel_ref[:, 0, t].reshape(depth, blocks * lanes)
        term = jnp.dot(
            cells_ref[:, t * depth : (t + 1) * depth], tap, preferred_element_type=jnp.float32
        )
        total = term if total is None else total + term
    for p in range(parts):
        for j in range(blocks):
            piece = total[p * size : (p + 1) * size, j * lanes : (j + 1) * lanes]
            out_ref[p, j] = piece.astype(out_ref.dtype)


def conv(cells, gathered, which, parts):
    owners, _, taps, rows, outs = gathered.shape
    size, lanes, step = cells.shape[0] // parts, 128, 2
    return pl.pallas_call(
        taps_kernel,
        grid=(outs // (lanes * step),),
        in_specs=[
            pl.BlockSpec(cells.shape, lambda n: (0, 0)),
            pl.BlockSpec(
                (owners, 1, taps, rows, lanes * step), lambda n: (0, which, 0, 0, n)
            ),
        ],
        out_specs=pl.BlockSpec((parts, step, size, lanes), lambda n: (0, n, 0, 0)),
        out_shape=jax.ShapeDtypeStruct((parts, outs // lanes, size, lanes), jnp.bfloat16),
        cost_estimate=pl.CostEstimate(
            flops=2 * cells.size * outs,
            bytes_accessed=2 * (cells.size + taps * owners * rows * outs),
            transcendentals=0,
        ),
    )(cells, gathered)


def body(features, kernel_one, bias_one, kernel_two, bias_two):
    lat = lax.axis_size("x") * lax.axis_size("ylo")
    lon = lax.axis_size("z") * lax.axis_size("core")
    x, ylo = lax.axis_index("x"), lax.axis_index("ylo")
    own = features[0]
    height, breadth, width = own.shape

    both = jnp.stack([half_of(kernel_one, ylo), half_of(kernel_two, ylo)])
    both = lax.all_gather(both, LON)

    ext = region(silu(own), lat, lon)
    top, bottom = x == 0, x == lax.axis_size("x") - 1
    last = ext.shape[0] - 1

    def rows_of(a):
        first = jnp.where(top, ext[2 - a : 3 - a], ext[a : a + 1])
        final = jnp.where(bottom, ext[last - a : last - a + 1], ext[last - 2 + a : last - 1 + a])
        return jnp.concatenate([first, ext[a + 1 : last - 2 + a], final])

    partial_one = conv(columns_of(rows_of, breadth + 2), both, 0, 1)[0]
    parts = lax.all_to_all(partial_one, "ch", 0, 0)
    hidden = parts.astype(jnp.float32).sum(0)
    hidden = hidden + jnp.where(ylo == 0, bias_one[: width // 2], bias_one[width // 2 :])
    mine = silu(hidden)
    other = lax.ppermute(mine, "ylo", [(0, 1), (1, 0)])
    act = jnp.concatenate(
        [jnp.where(ylo == 0, mine, other), jnp.where(ylo == 0, other, mine)], axis=1
    )
    act = act.reshape(2 * height + 2, breadth + 2, width)

    cells = columns_of(lambda a: act[a : a + 2 * height], breadth)
    partial_two = conv(cells, both, 1, 2).reshape(8, height * breadth, width // 2)
    parts = lax.all_to_all(partial_two, ("ylo", "ch"), 0, 0)
    second = parts.astype(jnp.float32).reshape(2, 4, height * breadth, width // 2).sum(1)
    second = jnp.concatenate([second[0], second[1]], axis=1) + bias_two
    second = second.reshape(height, breadth, width)
    return ((own.astype(jnp.float32) + second) * skip_scale).astype(jnp.bfloat16)[None]


def solution(mesh):
    lat, lon, ch = (mesh.shape[name] for name in ("lat", "lon", "ch"))
    fine = Mesh(mesh.devices.reshape(lat // 2, 2, lon // 2, 2, ch), AXES)
    field = P(None, LAT, LON, "ch")
    kernel = P(None, None, "ch", LON, None)
    return jax.shard_map(
        body,
        mesh=fine,
        in_specs=(field, kernel, P("ch"), kernel, P("ch")),
        out_specs=field,
        check_vma=False,
    )
```

```python
import jax
import jax.numpy as jnp
from jax import lax
from jax.sharding import Mesh, PartitionSpec as P

skip_scale = 0.7071067811865476
AXES = ("xh", "xl", "ylo", "z", "core", "ch")
LAT, LON, QUAD = ("xh", "xl", "ylo"), ("z", "core"), ("xl", "ylo")
SWAP = [(0, 1), (1, 0)]
LANES = 128
SLICE = 64


def silu(v):
    return jax.nn.silu(v.astype(jnp.float32)).astype(jnp.bfloat16)


def quarter(kernel, member, groups):
    taps, rows, outs = 9, kernel.shape[3], kernel.shape[4]
    column = lax.broadcasted_iota(jnp.int32, (outs, groups * SLICE), 1)
    wanted = column // SLICE * (outs // groups) + member * SLICE + column % SLICE
    pick = lax.broadcasted_iota(jnp.int32, wanted.shape, 0) == wanted
    flat = kernel.reshape(taps * rows, outs)
    chosen = jnp.dot(flat, pick.astype(flat.dtype), preferred_element_type=jnp.float32)
    return chosen.astype(flat.dtype).reshape(taps, rows, groups * SLICE)


def copies_of(block):
    return jnp.broadcast_to(block[None], (lax.axis_size("z"),) + block.shape)


def reduced(blocks, axis):
    me, count = lax.axis_index(axis), blocks.shape[0]
    total = lax.dynamic_index_in_dim(blocks, me, 0, keepdims=False).astype(jnp.float32)
    for d in range(1, count):
        sent = lax.dynamic_index_in_dim(blocks, lax.rem(me + d, count), 0, keepdims=False)
        came = lax.ppermute(sent, axis, [(i, (i + d) % count) for i in range(count)])
        total = total + came.astype(jnp.float32)
    return total


def from_quad(block):
    came = [block]
    for d in range(1, 4):
        came.append(lax.ppermute(block, QUAD, [(i, i ^ d) for i in range(4)]))
    return came


def lon_halo(block, width, lon):
    up = [(i, (i + 1) % lon) for i in range(lon)]
    down = [(j, i) for i, j in up]
    before = lax.ppermute(block[:, -width:], LON, up)
    after = lax.ppermute(block[:, :width], LON, down)
    return jnp.concatenate([before, block, after], axis=1)


def edge_pairs(lat, lon, far):
    pairs = []
    for i in range(lat):
        if i % 4 not in (0, 3):
            continue
        k = i - 1 if i % 4 == 0 else i + 1
        for j in range(lon):
            to = (k, j) if 0 <= k < lat else (i, (j + lon // 2) % lon)
            band = to[0] ^ 1 if far else to[0]
            pairs.append((i * lon + j, band * lon + to[1]))
    return pairs


def region(block, member, upper, lon):
    sent = jnp.where(member == 3, block[-2:], block[:2])
    near, far = (lax.ppermute(sent, LAT + LON, edge_pairs(8, lon, f)) for f in (False, True))
    past = jnp.where((member == 0) | (member == 3), near, far)
    past = jnp.where(upper == (member < 2), past[::-1], past)
    other = lax.ppermute(block, "ylo", SWAP)
    odd = member % 2 == 1
    both = [jnp.where(odd, other, block), jnp.where(odd, block, other), past]
    both = jnp.concatenate(both)
    other = lax.ppermute(both, "xl", SWAP)
    low, high = jnp.where(member < 2, both, other), jnp.where(member < 2, other, both)
    inner = 2 * block.shape[0]
    return jnp.concatenate([low[inner:], low[:inner], high])


def with_rims(ext, upper):
    first, final = ext[:3], ext[-3:]
    first = jnp.where(upper, first[::-1], first)
    final = jnp.where(upper, final, final[::-1])
    return jnp.concatenate([first, ext[1:-1], final])


def conv(cells, mine, other, core):
    low, high = jnp.where(core == 0, mine, other), jnp.where(core == 0, other, mine)
    kernel = jnp.stack([low, high], axis=1).transpose(2, 0, 1, 3, 4)
    kernel = kernel.reshape(3, 3, cells.shape[2], mine.shape[3])
    out = lax.conv_general_dilated(
        cells[None],
        kernel,
        (1, 1),
        "VALID",
        dimension_numbers=("NHWC", "HWIO", "NHWC"),
        preferred_element_type=jnp.float32,
    )
    return out[0].astype(jnp.bfloat16)


def folded(low, high):
    groups = low.shape[1] // SLICE
    cut = [slice(g * SLICE, (g + 1) * SLICE) for g in range(groups)]
    return jnp.stack([jnp.concatenate([low[:, c], high[:, c]], axis=1) for c in cut])


def body(features, kernel_one, bias_one, kernel_two, bias_two):
    lon = lax.axis_size("z") * lax.axis_size("core")
    groups = lax.axis_size("ch")
    member = lax.axis_index(QUAD).astype(jnp.int32)
    upper = lax.axis_index("xh") == 0
    core = lax.axis_index("core")
    own = features[0]
    height, breadth, width = own.shape

    first = silu(own)
    block = copies_of(quarter(kernel_one, member, groups))
    block, first = lax.optimization_barrier((block, first))
    mine = lax.all_to_all(block, "z", 0, 0)
    ext = lon_halo(region(first, member, upper, lon), 2, lon)
    other = lax.ppermute(mine, "core", SWAP)
    out = conv(with_rims(ext, upper), mine, other, core)
    out = jnp.concatenate([out[:1], out[3:-3], out[-1:]])
    half = 2 * height + 2
    partial = folded(
        out[:half].reshape(-1, out.shape[2]), out[-half:].reshape(-1, out.shape[2])
    )

    block = copies_of(quarter(kernel_two, member, groups))
    block, partial = lax.optimization_barrier((block, partial))
    mine = lax.all_to_all(block, "z", 0, 0)
    bias = lax.dynamic_slice_in_dim(bias_one, member * SLICE, SLICE, 0)
    hidden = reduced(partial, "ch") + jnp.concatenate([bias, bias])
    hidden, mine = lax.optimization_barrier((hidden, mine))
    other = lax.ppermute(mine, "core", SWAP)
    acts = from_quad(silu(hidden))
    acts = jnp.stack(acts).reshape(4, half, breadth + 2, LANES)
    acts = [lax.dynamic_index_in_dim(acts, member ^ k, 0, keepdims=False) for k in range(4)]
    acts = [jnp.concatenate([a[:-1, :, :SLICE], a[1:, :, SLICE:]]) for a in acts]
    out = conv(jnp.concatenate(acts, axis=2), mine, other, core)
    out = out.reshape(4, height * breadth, groups * SLICE)
    out = jnp.pad(out, ((0, 0), (0, (8 - height) * breadth), (0, 0)))
    partial = jnp.stack([folded(o[: 4 * breadth], o[4 * breadth :]) for o in out])
    parts = lax.all_to_all(partial.reshape(4 * groups, -1, LANES), QUAD + ("ch",), 0, 0)
    parts = parts.astype(jnp.float32).reshape(4, groups, -1, LANES).sum(1)
    first, rest = parts[:, :, :SLICE], parts[:, : (height - 4) * breadth, SLICE:]
    second = jnp.concatenate([first, rest], axis=1)
    second = jnp.concatenate([second[k] for k in range(4)], axis=1) + bias_two
    second = second.reshape(height, breadth, width)
    return ((own.astype(jnp.float32) + second) * skip_scale).astype(jnp.bfloat16)[None]


def solution(mesh):
    lat, lon, ch = (mesh.shape[name] for name in ("lat", "lon", "ch"))
    fine = Mesh(mesh.devices.reshape(lat // 4, 2, 2, lon // 2, 2, ch), AXES)
    field = P(None, LAT, LON, "ch")
    kernel = P(None, None, "ch", LON, None)
    return jax.shard_map(
        body,
        mesh=fine,
        in_specs=(field, kernel, P("ch"), kernel, P("ch")),
        out_specs=field,
        check_vma=False,
    )
```

```python
import jax
import jax.numpy as jnp
from jax import lax
from jax.sharding import Mesh, PartitionSpec as P

skip_scale = 0.7071067811865476
AXES = ("xh", "xl", "ylo", "z", "core", "ch")
LAT, LON, QUAD = ("xh", "xl", "ylo"), ("z", "core"), ("xl", "ylo")
SWAP = [(0, 1), (1, 0)]
LANES = 128
SLICE = 64


def silu(v):
    return jax.nn.silu(v.astype(jnp.float32)).astype(jnp.bfloat16)


def quarter(kernel, member, groups):
    taps, rows, outs = 9, kernel.shape[3], kernel.shape[4]
    column = lax.broadcasted_iota(jnp.int32, (outs, groups * SLICE), 1)
    wanted = column // SLICE * (outs // groups) + member * SLICE + column % SLICE
    pick = lax.broadcasted_iota(jnp.int32, wanted.shape, 0) == wanted
    flat = kernel.reshape(taps * rows, outs)
    chosen = jnp.dot(flat, pick.astype(flat.dtype), preferred_element_type=jnp.float32)
    return chosen.astype(flat.dtype).reshape(taps, rows, groups * SLICE)


def copies_of(block):
    return jnp.broadcast_to(block[None], (lax.axis_size("z"),) + block.shape)


def reduced(blocks, axis):
    me, count = lax.axis_index(axis), blocks.shape[0]
    total = lax.dynamic_index_in_dim(blocks, me, 0, keepdims=False).astype(jnp.float32)
    for d in range(1, count):
        sent = lax.dynamic_index_in_dim(blocks, lax.rem(me + d, count), 0, keepdims=False)
        came = lax.ppermute(sent, axis, [(i, (i + d) % count) for i in range(count)])
        total = total + came.astype(jnp.float32)
    return total


def from_quad(block, member):
    blocks = block[None]
    for axis, later in (("ylo", member % 2 == 1), ("xl", member >= 2)):
        other = lax.ppermute(blocks, axis, SWAP)
        blocks = jnp.concatenate(
            [jnp.where(later, other, blocks), jnp.where(later, blocks, other)]
        )
    return blocks


def lon_halo(block, width, lon):
    up = [(i, (i + 1) % lon) for i in range(lon)]
    down = [(j, i) for i, j in up]
    before = lax.ppermute(block[:, -width:], LON, up)
    after = lax.ppermute(block[:, :width], LON, down)
    return jnp.concatenate([before, block, after], axis=1)


def edge_pairs(lat, lon, far):
    pairs = []
    for i in range(lat):
        if i % 4 not in (0, 3):
            continue
        k = i - 1 if i % 4 == 0 else i + 1
        for j in range(lon):
            to = (k, j) if 0 <= k < lat else (i, (j + lon // 2) % lon)
            band = to[0] ^ 1 if far else to[0]
            pairs.append((i * lon + j, band * lon + to[1]))
    return pairs


def region(block, member, upper, lon):
    sent = jnp.where(member == 3, block[-2:], block[:2])
    near, far = (lax.ppermute(sent, LAT + LON, edge_pairs(8, lon, f)) for f in (False, True))
    past = jnp.where((member == 0) | (member == 3), near, far)
    past = jnp.where(upper == (member < 2), past[::-1], past)
    other = lax.ppermute(block, "ylo", SWAP)
    odd = member % 2 == 1
    both = [jnp.where(odd, other, block), jnp.where(odd, block, other), past]
    both = jnp.concatenate(both)
    other = lax.ppermute(both, "xl", SWAP)
    low, high = jnp.where(member < 2, both, other), jnp.where(member < 2, other, both)
    inner = 2 * block.shape[0]
    return jnp.concatenate([low[inner:], low[:inner], high])


def with_rims(ext, upper):
    first, final = ext[:3], ext[-3:]
    first = jnp.where(upper, first[::-1], first)
    final = jnp.where(upper, final, final[::-1])
    return jnp.concatenate([first, ext[1:-1], final])


def conv(cells, mine, other, core):
    low, high = jnp.where(core == 0, mine, other), jnp.where(core == 0, other, mine)
    kernel = jnp.stack([low, high], axis=1).transpose(2, 0, 1, 3, 4)
    kernel = kernel.reshape(3, 3, cells.shape[2], mine.shape[3])
    out = lax.conv_general_dilated(
        cells[None],
        kernel,
        (1, 1),
        "VALID",
        dimension_numbers=("NHWC", "HWIO", "NHWC"),
        preferred_element_type=jnp.float32,
    )
    return out[0].astype(jnp.bfloat16)


def folded(cells, size):
    short = 2 * size - cells.shape[-2]
    low, high = cells[..., :size, :], cells[..., size:, :]
    high = jnp.pad(high, [(0, 0)] * (cells.ndim - 2) + [(0, short), (0, 0)])
    cut = [slice(g * SLICE, (g + 1) * SLICE) for g in range(cells.shape[-1] // SLICE)]
    return jnp.stack([jnp.concatenate([low[..., c], high[..., c]], -1) for c in cut], -3)


def unfolded(blocks, count):
    size = blocks.shape[-2]
    low, high = blocks[..., :SLICE], blocks[..., : count - size, SLICE:]
    return jnp.concatenate([low, high], -2)


def half_of(count):
    return -(-count // 16) * 8


def body(features, kernel_one, bias_one, kernel_two, bias_two):
    lon = lax.axis_size("z") * lax.axis_size("core")
    groups = lax.axis_size("ch")
    member = lax.axis_index(QUAD).astype(jnp.int32)
    upper = lax.axis_index("xh") == 0
    core = lax.axis_index("core")
    own = features[0]
    height, breadth, width = own.shape

    first = silu(own)
    block = copies_of(quarter(kernel_one, member, groups))
    block, first = lax.optimization_barrier((block, first))
    mine = lax.all_to_all(block, "z", 0, 0)
    ext = region(first, member, upper, lon)
    block, ext = lax.optimization_barrier((copies_of(quarter(kernel_two, member, groups)), ext))
    ext = lon_halo(ext, 2, lon)
    other = lax.ppermute(mine, "core", SWAP)
    out = conv(with_rims(ext, upper), mine, other, core)
    out = jnp.concatenate([out[:1], out[3:-3], out[-1:]])
    rows, columns = out.shape[0], out.shape[1]
    count = rows * columns
    partial = folded(out.reshape(count, -1), half_of(count))

    block, partial = lax.optimization_barrier((block, partial))
    mine = lax.all_to_all(block, "z", 0, 0)
    bias = lax.dynamic_slice_in_dim(bias_one, member * SLICE, SLICE, 0)
    hidden = reduced(partial, "ch") + jnp.concatenate([bias, bias])
    hidden, mine = lax.optimization_barrier((hidden, mine))
    other = lax.ppermute(mine, "core", SWAP)
    acts = unfolded(from_quad(silu(hidden), member), count)
    acts = jnp.concatenate([acts[k] for k in range(4)], axis=1)
    out = conv(acts.reshape(rows, columns, -1), mine, other, core)
    count = height * breadth
    partial = folded(out.reshape(4, count, -1), half_of(count))
    parts = lax.all_to_all(partial.reshape(4 * groups, -1, LANES), QUAD + ("ch",), 0, 0)
    parts = parts.astype(jnp.float32).reshape(4, groups, -1, LANES).sum(1)
    second = unfolded(parts, count)
    second = jnp.concatenate([second[k] for k in range(4)], axis=1) + bias_two
    second = second.reshape(height, breadth, width)
    return ((own.astype(jnp.float32) + second) * skip_scale).astype(jnp.bfloat16)[None]


def solution(mesh):
    lat, lon, ch = (mesh.shape[name] for name in ("lat", "lon", "ch"))
    fine = Mesh(mesh.devices.reshape(lat // 4, 2, 2, lon // 2, 2, ch), AXES)
    field = P(None, LAT, LON, "ch")
    kernel = P(None, None, "ch", LON, None)
    return jax.shard_map(
        body,
        mesh=fine,
        in_specs=(field, kernel, P("ch"), kernel, P("ch")),
        out_specs=field,
        check_vma=False,
    )
```

```python
import jax
import jax.numpy as jnp
from jax import lax
from jax.sharding import Mesh, PartitionSpec as P

skip_scale = 0.7071067811865476
AXES = ("xh", "xl", "ylo", "z", "core", "ch")
LAT, LON, QUAD = ("xh", "xl", "ylo"), ("z", "core"), ("xl", "ylo")
SWAP = [(0, 1), (1, 0)]
LANES = 128
SLICE = 64


def silu(v):
    return jax.nn.silu(v.astype(jnp.float32)).astype(jnp.bfloat16)


def quarter(kernel, member, groups):
    taps, rows, outs = 9, kernel.shape[3], kernel.shape[4]
    column = lax.broadcasted_iota(jnp.int32, (outs, groups * SLICE), 1)
    wanted = column // SLICE * (outs // groups) + member * SLICE + column % SLICE
    pick = lax.broadcasted_iota(jnp.int32, wanted.shape, 0) == wanted
    flat = kernel.reshape(taps * rows, outs)
    chosen = jnp.dot(flat, pick.astype(flat.dtype), preferred_element_type=jnp.float32)
    return chosen.astype(flat.dtype).reshape(taps, rows, groups * SLICE)


def copies_of(block):
    return jnp.broadcast_to(block[None], (lax.axis_size("z"),) + block.shape)


def reduced(blocks, axis):
    me, count = lax.axis_index(axis), blocks.shape[0]
    total = lax.dynamic_index_in_dim(blocks, me, 0, keepdims=False).astype(jnp.float32)
    for d in range(1, count):
        sent = lax.dynamic_index_in_dim(blocks, lax.rem(me + d, count), 0, keepdims=False)
        came = lax.ppermute(sent, axis, [(i, (i + d) % count) for i in range(count)])
        total = total + came.astype(jnp.float32)
    return total


def lon_halo(block, width, lon):
    up = [(i, (i + 1) % lon) for i in range(lon)]
    down = [(j, i) for i, j in up]
    before = lax.ppermute(block[:, -width:], LON, up)
    after = lax.ppermute(block[:, :width], LON, down)
    return jnp.concatenate([before, block, after], axis=1)


def edge_pairs(lat, lon, far):
    pairs = []
    for i in range(lat):
        if i % 4 not in (0, 3):
            continue
        k = i - 1 if i % 4 == 0 else i + 1
        for j in range(lon):
            to = (k, j) if 0 <= k < lat else (i, (j + lon // 2) % lon)
            band = to[0] ^ 1 if far else to[0]
            pairs.append((i * lon + j, band * lon + to[1]))
    return pairs


def region(block, member, upper, lon):
    sent = jnp.where(member == 3, block[-2:], block[:2])
    near, far = (lax.ppermute(sent, LAT + LON, edge_pairs(8, lon, f)) for f in (False, True))
    past = jnp.where((member == 0) | (member == 3), near, far)
    past = jnp.where(upper == (member < 2), past[::-1], past)
    other = lax.ppermute(block, "ylo", SWAP)
    odd = member % 2 == 1
    both = [jnp.where(odd, other, block), jnp.where(odd, block, other), past]
    both = jnp.concatenate(both)
    other = lax.ppermute(both, "xl", SWAP)
    low, high = jnp.where(member < 2, both, other), jnp.where(member < 2, other, both)
    inner = 2 * block.shape[0]
    return jnp.concatenate([low[inner:], low[:inner], high])


def with_rims(ext, upper):
    first, final = ext[:3], ext[-3:]
    first = jnp.where(upper, first[::-1], first)
    final = jnp.where(upper, final, final[::-1])
    return jnp.concatenate([first, ext[1:-1], final])


def conv(cells, mine, other, core):
    low, high = jnp.where(core == 0, mine, other), jnp.where(core == 0, other, mine)
    kernel = jnp.stack([low, high], axis=1).transpose(2, 0, 1, 3, 4)
    kernel = kernel.reshape(3, 3, cells.shape[2], mine.shape[3])
    out = lax.conv_general_dilated(
        cells[None],
        kernel,
        (1, 1),
        "VALID",
        dimension_numbers=("NHWC", "HWIO", "NHWC"),
        preferred_element_type=jnp.float32,
    )
    return out[0].astype(jnp.bfloat16)


def folded(cells, size):
    short = 2 * size - cells.shape[-2]
    low, high = cells[..., :size, :], cells[..., size:, :]
    high = jnp.pad(high, [(0, 0)] * (cells.ndim - 2) + [(0, short), (0, 0)])
    cut = [slice(g * SLICE, (g + 1) * SLICE) for g in range(cells.shape[-1] // SLICE)]
    return jnp.stack([jnp.concatenate([low[..., c], high[..., c]], -1) for c in cut], -3)


def unfolded(blocks, count):
    size = blocks.shape[-2]
    low, high = blocks[..., :SLICE], blocks[..., : count - size, SLICE:]
    return jnp.concatenate([low, high], -2)


def half_of(count):
    return -(-count // 16) * 8


def body(features, kernel_one, bias_one, kernel_two, bias_two):
    lon = lax.axis_size("z") * lax.axis_size("core")
    groups = lax.axis_size("ch")
    member = lax.axis_index(QUAD).astype(jnp.int32)
    upper = lax.axis_index("xh") == 0
    core = lax.axis_index("core")
    own = features[0]
    height, breadth, width = own.shape

    block = copies_of(quarter(kernel_one, member, groups))
    mine = lax.all_to_all(block, "z", 0, 0)
    ext = region(own, member, upper, lon)
    rims = with_rims(silu(lon_halo(ext, 2, lon)), upper)
    block, rims = lax.optimization_barrier((copies_of(quarter(kernel_two, member, groups)), rims))
    mine_two = lax.all_to_all(block, "z", 0, 0)
    other = lax.ppermute(mine, "core", SWAP)
    out = conv(rims, mine, other, core)
    out = jnp.concatenate([out[:1], out[3:-3], out[-1:]])
    rows, columns = out.shape[0], out.shape[1]
    count = rows * columns
    partial = folded(out.reshape(count, -1), half_of(count))

    mine = mine_two
    bias = lax.dynamic_slice_in_dim(bias_one, member * SLICE, SLICE, 0)
    hidden = reduced(partial, "ch") + jnp.concatenate([bias, bias])
    acts = jnp.broadcast_to(silu(hidden), (4,) + hidden.shape)
    acts, mine = lax.optimization_barrier((acts, mine))
    other = lax.ppermute(mine, "core", SWAP)
    acts = unfolded(lax.all_to_all(acts, QUAD, 0, 0), count)
    acts = jnp.concatenate([acts[k] for k in range(4)], axis=1)
    out = conv(acts.reshape(rows, columns, -1), mine, other, core)
    count = height * breadth
    partial = folded(out.reshape(4, count, -1), half_of(count))
    parts = lax.all_to_all(partial.reshape(4 * groups, -1, LANES), QUAD + ("ch",), 0, 0)
    parts = parts.astype(jnp.float32).reshape(4, groups, -1, LANES).sum(1)
    second = unfolded(parts, count)
    second = jnp.concatenate([second[k] for k in range(4)], axis=1) + bias_two
    second = second.reshape(height, breadth, width)
    return ((own.astype(jnp.float32) + second) * skip_scale).astype(jnp.bfloat16)[None]


def solution(mesh):
    lat, lon, ch = (mesh.shape[name] for name in ("lat", "lon", "ch"))
    fine = Mesh(mesh.devices.reshape(lat // 4, 2, 2, lon // 2, 2, ch), AXES)
    field = P(None, LAT, LON, "ch")
    kernel = P(None, None, "ch", LON, None)
    return jax.shard_map(
        body,
        mesh=fine,
        in_specs=(field, kernel, P("ch"), kernel, P("ch")),
        out_specs=field,
        check_vma=False,
    )
```

```python
import jax
import jax.numpy as jnp
from jax import lax
from jax.sharding import Mesh, PartitionSpec as P

skip_scale = 0.7071067811865476
AXES = ("xh", "xl", "ylo", "z", "core", "ch")
LAT, LON, QUAD = ("xh", "xl", "ylo"), ("z", "core"), ("xl", "ylo")
SWAP = [(0, 1), (1, 0)]
LANES = 128
SLICE = 64


def silu(v):
    return jax.nn.silu(v.astype(jnp.float32)).astype(jnp.bfloat16)


def quarter(kernel, member, groups):
    taps, rows, outs = 9, kernel.shape[3], kernel.shape[4]
    column = lax.broadcasted_iota(jnp.int32, (outs, groups * SLICE), 1)
    wanted = column // SLICE * (outs // groups) + member * SLICE + column % SLICE
    pick = lax.broadcasted_iota(jnp.int32, wanted.shape, 0) == wanted
    flat = kernel.reshape(taps * rows, outs)
    chosen = jnp.dot(flat, pick.astype(flat.dtype), preferred_element_type=jnp.float32)
    return chosen.astype(flat.dtype).reshape(taps, rows, groups * SLICE)


def copies_of(block):
    return jnp.broadcast_to(block[None], (lax.axis_size("z"),) + block.shape)


def traded(blocks, axis):
    me, count = lax.axis_index(axis), blocks.shape[0]
    came = [lax.dynamic_index_in_dim(blocks, me, 0, keepdims=False)]
    for d in range(1, count):
        sent = lax.dynamic_index_in_dim(blocks, lax.rem(me + d, count), 0, keepdims=False)
        came.append(lax.ppermute(sent, axis, [(i, (i + d) % count) for i in range(count)]))
    return came


def from_quad(block, member):
    blocks = block[None]
    for axis, later in (("ylo", member % 2 == 1), ("xl", member >= 2)):
        other = lax.ppermute(blocks, axis, SWAP)
        blocks = jnp.concatenate(
            [jnp.where(later, other, blocks), jnp.where(later, blocks, other)]
        )
    return blocks


def lon_halo(block, width, lon):
    up = [(i, (i + 1) % lon) for i in range(lon)]
    down = [(j, i) for i, j in up]
    before = lax.ppermute(block[:, -width:], LON, up)
    after = lax.ppermute(block[:, :width], LON, down)
    return jnp.concatenate([before, block, after], axis=1)


def edge_pairs(lat, lon, far):
    pairs = []
    for i in range(lat):
        if i % 4 not in (0, 3):
            continue
        k = i - 1 if i % 4 == 0 else i + 1
        for j in range(lon):
            to = (k, j) if 0 <= k < lat else (i, (j + lon // 2) % lon)
            band = to[0] ^ 1 if far else to[0]
            pairs.append((i * lon + j, band * lon + to[1]))
    return pairs


def region(block, member, upper, lon):
    sent = jnp.where(member == 3, block[-2:], block[:2])
    near, far = (lax.ppermute(sent, LAT + LON, edge_pairs(8, lon, f)) for f in (False, True))
    past = jnp.where((member == 0) | (member == 3), near, far)
    past = jnp.where(upper == (member < 2), past[::-1], past)
    other = lax.ppermute(block, "ylo", SWAP)
    odd = member % 2 == 1
    both = [jnp.where(odd, other, block), jnp.where(odd, block, other), past]
    both = jnp.concatenate(both)
    other = lax.ppermute(both, "xl", SWAP)
    low, high = jnp.where(member < 2, both, other), jnp.where(member < 2, other, both)
    inner = 2 * block.shape[0]
    return jnp.concatenate([low[inner:], low[:inner], high])


def with_rims(ext, upper):
    first, final = ext[:3], ext[-3:]
    first = jnp.where(upper, first[::-1], first)
    final = jnp.where(upper, final, final[::-1])
    return jnp.concatenate([first, ext[1:-1], final])


def conv(cells, mine, other, core):
    low, high = jnp.where(core == 0, mine, other), jnp.where(core == 0, other, mine)
    kernel = jnp.stack([low, high], axis=1).transpose(2, 0, 1, 3, 4)
    kernel = kernel.reshape(3, 3, cells.shape[2], mine.shape[3])
    out = lax.conv_general_dilated(
        cells[None],
        kernel,
        (1, 1),
        "VALID",
        dimension_numbers=("NHWC", "HWIO", "NHWC"),
        preferred_element_type=jnp.float32,
    )
    return out[0].astype(jnp.bfloat16)


def folded(cells, size):
    short = 2 * size - cells.shape[-2]
    low, high = cells[..., :size, :], cells[..., size:, :]
    high = jnp.pad(high, [(0, 0)] * (cells.ndim - 2) + [(0, short), (0, 0)])
    cut = [slice(g * SLICE, (g + 1) * SLICE) for g in range(cells.shape[-1] // SLICE)]
    return jnp.stack([jnp.concatenate([low[..., c], high[..., c]], -1) for c in cut], -3)


def unfolded(blocks, count):
    size = blocks.shape[-2]
    low, high = blocks[..., :SLICE], blocks[..., : count - size, SLICE:]
    return jnp.concatenate([low, high], -2)


def half_of(count):
    return -(-count // 16) * 8


def body(features, kernel_one, bias_one, kernel_two, bias_two):
    lon = lax.axis_size("z") * lax.axis_size("core")
    groups = lax.axis_size("ch")
    member = lax.axis_index(QUAD).astype(jnp.int32)
    upper = lax.axis_index("xh") == 0
    core = lax.axis_index("core")
    own = features[0]
    height, breadth, width = own.shape

    block = copies_of(quarter(kernel_one, member, groups))
    mine = lax.all_to_all(block, "z", 0, 0)
    ext = region(own, member, upper, lon)
    ext = silu(lon_halo(ext, 2, lon))
    other = lax.ppermute(mine, "core", SWAP)
    out = conv(with_rims(ext, upper), mine, other, core)
    out = jnp.concatenate([out[:1], out[3:-3], out[-1:]])
    rows, columns = out.shape[0], out.shape[1]
    count = rows * columns
    partial = folded(out.reshape(count, -1), half_of(count))

    came = traded(partial, "ch")
    block = copies_of(quarter(kernel_two, member, groups))
    block, came[3] = lax.optimization_barrier((block, came[3]))
    mine = lax.all_to_all(block, "z", 0, 0)
    bias = lax.dynamic_slice_in_dim(bias_one, member * SLICE, SLICE, 0)
    hidden = sum(part.astype(jnp.float32) for part in came) + jnp.concatenate([bias, bias])
    acts, mine = lax.optimization_barrier((from_quad(silu(hidden), member), mine))
    other = lax.ppermute(mine, "core", SWAP)
    acts = unfolded(acts, count)
    acts = jnp.concatenate([acts[k] for k in range(4)], axis=1)
    out = conv(acts.reshape(rows, columns, -1), mine, other, core)
    count = height * breadth
    partial = folded(out.reshape(4, count, -1), half_of(count))
    parts = lax.all_to_all(partial.reshape(4 * groups, -1, LANES), QUAD + ("ch",), 0, 0)
    parts = parts.astype(jnp.float32).reshape(4, groups, -1, LANES).sum(1)
    second = unfolded(parts, count)
    second = jnp.concatenate([second[k] for k in range(4)], axis=1) + bias_two
    second = second.reshape(height, breadth, width)
    return ((own.astype(jnp.float32) + second) * skip_scale).astype(jnp.bfloat16)[None]


def solution(mesh):
    lat, lon, ch = (mesh.shape[name] for name in ("lat", "lon", "ch"))
    fine = Mesh(mesh.devices.reshape(lat // 4, 2, 2, lon // 2, 2, ch), AXES)
    field = P(None, LAT, LON, "ch")
    kernel = P(None, None, "ch", LON, None)
    return jax.shard_map(
        body,
        mesh=fine,
        in_specs=(field, kernel, P("ch"), kernel, P("ch")),
        out_specs=field,
        check_vma=False,
    )
```

```python
import jax
import jax.numpy as jnp
from jax import lax
from jax.sharding import Mesh, PartitionSpec as P

skip_scale = 0.7071067811865476
AXES = ("xh", "xl", "ylo", "z", "core", "ch")
LAT, LON, QUAD = ("xh", "xl", "ylo"), ("z", "core"), ("xl", "ylo")
SWAP = [(0, 1), (1, 0)]
LANES = 128
SLICE = 64


def silu(v):
    return jax.nn.silu(v.astype(jnp.float32)).astype(jnp.bfloat16)


def quarter(kernel, member, groups):
    taps, rows, outs = 9, kernel.shape[3], kernel.shape[4]
    column = lax.broadcasted_iota(jnp.int32, (outs, groups * SLICE), 1)
    wanted = column // SLICE * (outs // groups) + member * SLICE + column % SLICE
    pick = lax.broadcasted_iota(jnp.int32, wanted.shape, 0) == wanted
    flat = kernel.reshape(taps * rows, outs)
    chosen = jnp.dot(flat, pick.astype(flat.dtype), preferred_element_type=jnp.float32)
    return chosen.astype(flat.dtype).reshape(taps, rows, groups * SLICE)


def copies_of(block):
    return jnp.broadcast_to(block[None], (lax.axis_size("z"),) + block.shape)


def traded(blocks, axis):
    me, count = lax.axis_index(axis), blocks.shape[0]
    came = [lax.dynamic_index_in_dim(blocks, me, 0, keepdims=False)]
    for d in range(1, count):
        sent = lax.dynamic_index_in_dim(blocks, lax.rem(me + d, count), 0, keepdims=False)
        came.append(lax.ppermute(sent, axis, [(i, (i + d) % count) for i in range(count)]))
    return came


def from_quad(block, member):
    blocks = block[None]
    for axis, later in (("ylo", member % 2 == 1), ("xl", member >= 2)):
        other = lax.ppermute(blocks, axis, SWAP)
        blocks = jnp.concatenate(
            [jnp.where(later, other, blocks), jnp.where(later, blocks, other)]
        )
    return blocks


def lon_halo(block, width, lon):
    up = [(i, (i + 1) % lon) for i in range(lon)]
    down = [(j, i) for i, j in up]
    before = lax.ppermute(block[:, -width:], LON, up)
    after = lax.ppermute(block[:, :width], LON, down)
    return jnp.concatenate([before, block, after], axis=1)


def edge_pairs(lat, lon, far):
    pairs = []
    for i in range(lat):
        if i % 4 not in (0, 3):
            continue
        k = i - 1 if i % 4 == 0 else i + 1
        for j in range(lon):
            to = (k, j) if 0 <= k < lat else (i, (j + lon // 2) % lon)
            band = to[0] ^ 1 if far else to[0]
            pairs.append((i * lon + j, band * lon + to[1]))
    return pairs


def region(block, member, upper, lon):
    sent = jnp.where(member == 3, block[-2:], block[:2])
    near, far = (lax.ppermute(sent, LAT + LON, edge_pairs(8, lon, f)) for f in (False, True))
    past = jnp.where((member == 0) | (member == 3), near, far)
    past = jnp.where(upper == (member < 2), past[::-1], past)
    other = lax.ppermute(block, "ylo", SWAP)
    odd = member % 2 == 1
    both = [jnp.where(odd, other, block), jnp.where(odd, block, other), past]
    both = jnp.concatenate(both)
    other = lax.ppermute(both, "xl", SWAP)
    low, high = jnp.where(member < 2, both, other), jnp.where(member < 2, other, both)
    inner = 2 * block.shape[0]
    return jnp.concatenate([low[inner:], low[:inner], high])


def with_rims(ext, upper):
    first, final = ext[:3], ext[-3:]
    first = jnp.where(upper, first[::-1], first)
    final = jnp.where(upper, final, final[::-1])
    return jnp.concatenate([first, ext[1:-1], final])


def conv(cells, mine, other, core):
    low, high = jnp.where(core == 0, mine, other), jnp.where(core == 0, other, mine)
    kernel = jnp.stack([low, high], axis=1).transpose(2, 0, 1, 3, 4)
    kernel = kernel.reshape(3, 3, cells.shape[2], mine.shape[3])
    out = lax.conv_general_dilated(
        cells[None],
        kernel,
        (1, 1),
        "VALID",
        dimension_numbers=("NHWC", "HWIO", "NHWC"),
        preferred_element_type=jnp.float32,
    )
    return out[0].astype(jnp.bfloat16)


def folded(cells, size):
    short = 2 * size - cells.shape[-2]
    low, high = cells[..., :size, :], cells[..., size:, :]
    high = jnp.pad(high, [(0, 0)] * (cells.ndim - 2) + [(0, short), (0, 0)])
    cut = [slice(g * SLICE, (g + 1) * SLICE) for g in range(cells.shape[-1] // SLICE)]
    return jnp.stack([jnp.concatenate([low[..., c], high[..., c]], -1) for c in cut], -3)


def unfolded(blocks, count):
    size = blocks.shape[-2]
    low, high = blocks[..., :SLICE], blocks[..., : count - size, SLICE:]
    return jnp.concatenate([low, high], -2)


def half_of(count):
    return -(-count // 16) * 8


def body(features, kernel_one, bias_one, kernel_two, bias_two):
    lon = lax.axis_size("z") * lax.axis_size("core")
    groups = lax.axis_size("ch")
    member = lax.axis_index(QUAD).astype(jnp.int32)
    upper = lax.axis_index("xh") == 0
    core = lax.axis_index("core")
    own = features[0]
    height, breadth, width = own.shape

    block = copies_of(quarter(kernel_one, member, groups))
    mine = lax.all_to_all(block, "z", 0, 0)
    ext = region(own, member, upper, lon)
    ext = silu(lon_halo(ext, 2, lon))
    other = lax.ppermute(mine, "core", SWAP)
    out = conv(with_rims(ext, upper), mine, other, core)
    out = jnp.concatenate([out[:1], out[3:-3], out[-1:]])
    rows, columns = out.shape[0], out.shape[1]
    count = rows * columns
    partial = folded(out.reshape(count, -1), half_of(count))

    block = copies_of(quarter(kernel_two, member, groups))
    block, partial = lax.optimization_barrier((block, partial))
    came = traded(partial, "ch")
    block, came[3] = lax.optimization_barrier((block, came[3]))
    mine = lax.all_to_all(block, "z", 0, 0)
    bias = lax.dynamic_slice_in_dim(bias_one, member * SLICE, SLICE, 0)
    hidden = sum(part.astype(jnp.float32) for part in came) + jnp.concatenate([bias, bias])
    acts, mine = lax.optimization_barrier((from_quad(silu(hidden), member), mine))
    other = lax.ppermute(mine, "core", SWAP)
    acts = unfolded(acts, count)
    acts = jnp.concatenate([acts[k] for k in range(4)], axis=1)
    out = conv(acts.reshape(rows, columns, -1), mine, other, core)
    count = height * breadth
    partial = folded(out.reshape(4, count, -1), half_of(count)).swapaxes(0, 1)
    parts = lax.all_to_all(partial.reshape(4 * groups, -1, LANES), ("ch",) + QUAD, 0, 0)
    parts = parts.astype(jnp.float32).reshape(groups, 4, -1, LANES).sum(0)
    second = unfolded(parts, count)
    second = jnp.concatenate([second[k] for k in range(4)], axis=1) + bias_two
    second = second.reshape(height, breadth, width)
    return ((own.astype(jnp.float32) + second) * skip_scale).astype(jnp.bfloat16)[None]


def solution(mesh):
    lat, lon, ch = (mesh.shape[name] for name in ("lat", "lon", "ch"))
    fine = Mesh(mesh.devices.reshape(lat // 4, 2, 2, lon // 2, 2, ch), AXES)
    field = P(None, LAT, LON, "ch")
    kernel = P(None, None, "ch", LON, None)
    return jax.shard_map(
        body,
        mesh=fine,
        in_specs=(field, kernel, P("ch"), kernel, P("ch")),
        out_specs=field,
        check_vma=False,
    )
```

```python
import jax
import jax.numpy as jnp
from jax import lax
from jax.sharding import Mesh, PartitionSpec as P

skip_scale = 0.7071067811865476
AXES = ("xh", "xl", "ylo", "z", "core", "ch")
LAT, LON, QUAD = ("xh", "xl", "ylo"), ("z", "core"), ("xl", "ylo")
SWAP = [(0, 1), (1, 0)]
LANES = 128
SLICE = 64


def silu(v):
    return jax.nn.silu(v.astype(jnp.float32)).astype(jnp.bfloat16)


def quarter(kernel, member, groups):
    taps, rows, outs = 9, kernel.shape[3], kernel.shape[4]
    column = lax.broadcasted_iota(jnp.int32, (outs, groups * SLICE), 1)
    wanted = column // SLICE * (outs // groups) + member * SLICE + column % SLICE
    pick = lax.broadcasted_iota(jnp.int32, wanted.shape, 0) == wanted
    flat = kernel.reshape(taps * rows, outs)
    chosen = jnp.dot(flat, pick.astype(flat.dtype), preferred_element_type=jnp.float32)
    return chosen.astype(flat.dtype).reshape(taps, rows, groups * SLICE)


def copies_of(block):
    return jnp.broadcast_to(block[None], (lax.axis_size("z"),) + block.shape)


def traded(blocks, axis):
    me, count = lax.axis_index(axis), blocks.shape[0]
    came = [lax.dynamic_index_in_dim(blocks, me, 0, keepdims=False)]
    for d in range(1, count):
        sent = lax.dynamic_index_in_dim(blocks, lax.rem(me + d, count), 0, keepdims=False)
        came.append(lax.ppermute(sent, axis, [(i, (i + d) % count) for i in range(count)]))
    return came


def from_quad(block, member):
    blocks = block[None]
    for axis, later in (("ylo", member % 2 == 1), ("xl", member >= 2)):
        other = lax.ppermute(blocks, axis, SWAP)
        blocks = jnp.concatenate(
            [jnp.where(later, other, blocks), jnp.where(later, blocks, other)]
        )
    return blocks


def lon_halo(block, width, lon):
    up = [(i, (i + 1) % lon) for i in range(lon)]
    down = [(j, i) for i, j in up]
    before = lax.ppermute(block[:, -width:], LON, up)
    after = lax.ppermute(block[:, :width], LON, down)
    return jnp.concatenate([before, block, after], axis=1)


def edge_pairs(lat, lon, far):
    pairs = []
    for i in range(lat):
        if i % 4 not in (0, 3):
            continue
        k = i - 1 if i % 4 == 0 else i + 1
        for j in range(lon):
            to = (k, j) if 0 <= k < lat else (i, (j + lon // 2) % lon)
            band = to[0] ^ 1 if far else to[0]
            pairs.append((i * lon + j, band * lon + to[1]))
    return pairs


def region(block, member, upper, lon):
    sent = jnp.where(member == 3, block[-2:], block[:2])
    near, far = (lax.ppermute(sent, LAT + LON, edge_pairs(8, lon, f)) for f in (False, True))
    past = jnp.where((member == 0) | (member == 3), near, far)
    past = jnp.where(upper == (member < 2), past[::-1], past)
    other = lax.ppermute(block, "ylo", SWAP)
    odd = member % 2 == 1
    both = [jnp.where(odd, other, block), jnp.where(odd, block, other), past]
    both = jnp.concatenate(both)
    other = lax.ppermute(both, "xl", SWAP)
    low, high = jnp.where(member < 2, both, other), jnp.where(member < 2, other, both)
    inner = 2 * block.shape[0]
    return jnp.concatenate([low[inner:], low[:inner], high])


def with_rims(ext, upper):
    first, final = ext[:3], ext[-3:]
    first = jnp.where(upper, first[::-1], first)
    final = jnp.where(upper, final, final[::-1])
    return jnp.concatenate([first, ext[1:-1], final])


def conv(cells, mine, other, core):
    low, high = jnp.where(core == 0, mine, other), jnp.where(core == 0, other, mine)
    kernel = jnp.stack([low, high], axis=1).transpose(2, 0, 1, 3, 4)
    kernel = kernel.reshape(3, 3, cells.shape[2], mine.shape[3])
    out = lax.conv_general_dilated(
        cells[None],
        kernel,
        (1, 1),
        "VALID",
        dimension_numbers=("NHWC", "HWIO", "NHWC"),
        preferred_element_type=jnp.float32,
    )
    return out[0].astype(jnp.bfloat16)


def folded(cells, size):
    short = 2 * size - cells.shape[-2]
    low, high = cells[..., :size, :], cells[..., size:, :]
    high = jnp.pad(high, [(0, 0)] * (cells.ndim - 2) + [(0, short), (0, 0)])
    cut = [slice(g * SLICE, (g + 1) * SLICE) for g in range(cells.shape[-1] // SLICE)]
    return jnp.stack([jnp.concatenate([low[..., c], high[..., c]], -1) for c in cut], -3)


def unfolded(blocks, count):
    size = blocks.shape[-2]
    low, high = blocks[..., :SLICE], blocks[..., : count - size, SLICE:]
    return jnp.concatenate([low, high], -2)


def half_of(count):
    return -(-count // 16) * 8


def body(features, kernel_one, bias_one, kernel_two, bias_two):
    lon = lax.axis_size("z") * lax.axis_size("core")
    groups = lax.axis_size("ch")
    member = lax.axis_index(QUAD).astype(jnp.int32)
    upper = lax.axis_index("xh") == 0
    core = lax.axis_index("core")
    own = features[0]
    height, breadth, width = own.shape

    block = copies_of(quarter(kernel_one, member, groups))
    mine = lax.all_to_all(block, "z", 0, 0)
    ext = region(own, member, upper, lon)
    ext = silu(lon_halo(ext, 2, lon))
    other = lax.ppermute(mine, "core", SWAP)
    out = conv(with_rims(ext, upper), mine, other, core)
    out = jnp.concatenate([out[:1], out[3:-3], out[-1:]])
    rows, columns = out.shape[0], out.shape[1]
    count = rows * columns
    partial = folded(out.reshape(count, -1), half_of(count))

    block = copies_of(quarter(kernel_two, member, groups))
    block, partial = lax.optimization_barrier((block, partial))
    came = traded(partial, "ch")
    block, came[1] = lax.optimization_barrier((block, came[1]))
    mine = lax.all_to_all(block, "z", 0, 0)
    bias = lax.dynamic_slice_in_dim(bias_one, member * SLICE, SLICE, 0)
    hidden = sum(part.astype(jnp.float32) for part in came) + jnp.concatenate([bias, bias])
    acts, mine = lax.optimization_barrier((from_quad(silu(hidden), member), mine))
    other = lax.ppermute(mine, "core", SWAP)
    acts = unfolded(acts, count)
    acts = jnp.concatenate([acts[k] for k in range(4)], axis=1)
    out = conv(acts.reshape(rows, columns, -1), mine, other, core)
    count = height * breadth
    partial = folded(out.reshape(4, count, -1), half_of(count)).swapaxes(0, 1)
    parts = lax.all_to_all(partial.reshape(4 * groups, -1, LANES), ("ch",) + QUAD, 0, 0)
    parts = parts.astype(jnp.float32).reshape(groups, 4, -1, LANES).sum(0)
    second = unfolded(parts, count)
    second = jnp.concatenate([second[k] for k in range(4)], axis=1) + bias_two
    second = second.reshape(height, breadth, width)
    return ((own.astype(jnp.float32) + second) * skip_scale).astype(jnp.bfloat16)[None]


def solution(mesh):
    lat, lon, ch = (mesh.shape[name] for name in ("lat", "lon", "ch"))
    fine = Mesh(mesh.devices.reshape(lat // 4, 2, 2, lon // 2, 2, ch), AXES)
    field = P(None, LAT, LON, "ch")
    kernel = P(None, None, "ch", LON, None)
    return jax.shard_map(
        body,
        mesh=fine,
        in_specs=(field, kernel, P("ch"), kernel, P("ch")),
        out_specs=field,
        check_vma=False,
    )
```

```python
import jax
import jax.numpy as jnp
from jax import lax
from jax.sharding import Mesh, PartitionSpec as P

skip_scale = 0.7071067811865476
AXES = ("xh", "xl", "ylo", "z", "core", "ch")
LAT, LON, QUAD = ("xh", "xl", "ylo"), ("z", "core"), ("xl", "ylo")
SWAP = [(0, 1), (1, 0)]
LANES = 128
SLICE = 64


def silu(v):
    return jax.nn.silu(v.astype(jnp.float32)).astype(jnp.bfloat16)


def quarter(kernel, member, groups):
    taps, rows, outs = 9, kernel.shape[3], kernel.shape[4]
    column = lax.broadcasted_iota(jnp.int32, (outs, groups * SLICE), 1)
    wanted = column // SLICE * (outs // groups) + member * SLICE + column % SLICE
    pick = lax.broadcasted_iota(jnp.int32, wanted.shape, 0) == wanted
    flat = kernel.reshape(taps * rows, outs)
    chosen = jnp.dot(flat, pick.astype(flat.dtype), preferred_element_type=jnp.float32)
    return chosen.astype(flat.dtype).reshape(taps, rows, groups * SLICE)


def copies_of(block):
    return jnp.broadcast_to(block[None], (lax.axis_size("z"),) + block.shape)


def traded(blocks, axis):
    me, count = lax.axis_index(axis), blocks.shape[0]
    came = {0: lax.dynamic_index_in_dim(blocks, me, 0, keepdims=False)}
    for d in (1, 3, 2):
        sent = lax.dynamic_index_in_dim(blocks, lax.rem(me + d, count), 0, keepdims=False)
        came[d] = lax.ppermute(sent, axis, [(i, (i + d) % count) for i in range(count)])
    return came


def from_quad(block, member):
    blocks = block[None]
    for axis, later in (("ylo", member % 2 == 1), ("xl", member >= 2)):
        other = lax.ppermute(blocks, axis, SWAP)
        blocks = jnp.concatenate(
            [jnp.where(later, other, blocks), jnp.where(later, blocks, other)]
        )
    return blocks


def lon_halo(block, width, lon):
    up = [(i, (i + 1) % lon) for i in range(lon)]
    down = [(j, i) for i, j in up]
    before = lax.ppermute(block[:, -width:], LON, up)
    after = lax.ppermute(block[:, :width], LON, down)
    return jnp.concatenate([before, block, after], axis=1)


def edge_pairs(lat, lon, far):
    pairs = []
    for i in range(lat):
        if i % 4 not in (0, 3):
            continue
        k = i - 1 if i % 4 == 0 else i + 1
        for j in range(lon):
            to = (k, j) if 0 <= k < lat else (i, (j + lon // 2) % lon)
            band = to[0] ^ 1 if far else to[0]
            pairs.append((i * lon + j, band * lon + to[1]))
    return pairs


def region(block, member, upper, lon):
    sent = jnp.where(member == 3, block[-2:], block[:2])
    near, far = (lax.ppermute(sent, LAT + LON, edge_pairs(8, lon, f)) for f in (False, True))
    past = jnp.where((member == 0) | (member == 3), near, far)
    past = jnp.where(upper == (member < 2), past[::-1], past)
    other = lax.ppermute(block, "ylo", SWAP)
    odd = member % 2 == 1
    both = [jnp.where(odd, other, block), jnp.where(odd, block, other), past]
    both = jnp.concatenate(both)
    other = lax.ppermute(both, "xl", SWAP)
    low, high = jnp.where(member < 2, both, other), jnp.where(member < 2, other, both)
    inner = 2 * block.shape[0]
    return jnp.concatenate([low[inner:], low[:inner], high])


def with_rims(ext, upper):
    first, final = ext[:3], ext[-3:]
    first = jnp.where(upper, first[::-1], first)
    final = jnp.where(upper, final, final[::-1])
    return jnp.concatenate([first, ext[1:-1], final])


def conv(cells, mine, other, core):
    low, high = jnp.where(core == 0, mine, other), jnp.where(core == 0, other, mine)
    kernel = jnp.stack([low, high], axis=1).transpose(2, 0, 1, 3, 4)
    kernel = kernel.reshape(3, 3, cells.shape[2], mine.shape[3])
    out = lax.conv_general_dilated(
        cells[None],
        kernel,
        (1, 1),
        "VALID",
        dimension_numbers=("NHWC", "HWIO", "NHWC"),
        preferred_element_type=jnp.float32,
    )
    return out[0].astype(jnp.bfloat16)


def folded(cells, size):
    short = 2 * size - cells.shape[-2]
    low, high = cells[..., :size, :], cells[..., size:, :]
    high = jnp.pad(high, [(0, 0)] * (cells.ndim - 2) + [(0, short), (0, 0)])
    cut = [slice(g * SLICE, (g + 1) * SLICE) for g in range(cells.shape[-1] // SLICE)]
    return jnp.stack([jnp.concatenate([low[..., c], high[..., c]], -1) for c in cut], -3)


def unfolded(blocks, count):
    size = blocks.shape[-2]
    low, high = blocks[..., :SLICE], blocks[..., : count - size, SLICE:]
    return jnp.concatenate([low, high], -2)


def half_of(count):
    return -(-count // 16) * 8


def body(features, kernel_one, bias_one, kernel_two, bias_two):
    lon = lax.axis_size("z") * lax.axis_size("core")
    groups = lax.axis_size("ch")
    member = lax.axis_index(QUAD).astype(jnp.int32)
    upper = lax.axis_index("xh") == 0
    core = lax.axis_index("core")
    own = features[0]
    height, breadth, width = own.shape

    block = copies_of(quarter(kernel_one, member, groups))
    mine = lax.all_to_all(block, "z", 0, 0)
    ext = region(own, member, upper, lon)
    ext = silu(lon_halo(ext, 2, lon))
    other = lax.ppermute(mine, "core", SWAP)
    out = conv(with_rims(ext, upper), mine, other, core)
    out = jnp.concatenate([out[:1], out[3:-3], out[-1:]])
    rows, columns = out.shape[0], out.shape[1]
    count = rows * columns
    partial = folded(out.reshape(count, -1), half_of(count))

    block = copies_of(quarter(kernel_two, member, groups))
    block, partial = lax.optimization_barrier((block, partial))
    came = traded(partial, "ch")
    block, came[2] = lax.optimization_barrier((block, came[2]))
    mine = lax.all_to_all(block, "z", 0, 0)
    bias = lax.dynamic_slice_in_dim(bias_one, member * SLICE, SLICE, 0)
    hidden = sum(part.astype(jnp.float32) for part in came.values()) + jnp.concatenate([bias, bias])
    acts, mine = lax.optimization_barrier((from_quad(silu(hidden), member), mine))
    other = lax.ppermute(mine, "core", SWAP)
    acts = unfolded(acts, count)
    acts = jnp.concatenate([acts[k] for k in range(4)], axis=1)
    out = conv(acts.reshape(rows, columns, -1), mine, other, core)
    count = height * breadth
    partial = folded(out.reshape(4, count, -1), half_of(count)).swapaxes(0, 1)
    parts = lax.all_to_all(partial.reshape(4 * groups, -1, LANES), ("ch",) + QUAD, 0, 0)
    parts = parts.astype(jnp.float32).reshape(groups, 4, -1, LANES).sum(0)
    second = unfolded(parts, count)
    second = jnp.concatenate([second[k] for k in range(4)], axis=1) + bias_two
    second = second.reshape(height, breadth, width)
    return ((own.astype(jnp.float32) + second) * skip_scale).astype(jnp.bfloat16)[None]


def solution(mesh):
    lat, lon, ch = (mesh.shape[name] for name in ("lat", "lon", "ch"))
    fine = Mesh(mesh.devices.reshape(lat // 4, 2, 2, lon // 2, 2, ch), AXES)
    field = P(None, LAT, LON, "ch")
    kernel = P(None, None, "ch", LON, None)
    return jax.shard_map(
        body,
        mesh=fine,
        in_specs=(field, kernel, P("ch"), kernel, P("ch")),
        out_specs=field,
        check_vma=False,
    )
```
